128 devices in a mesh: row: 16 (over y_hi, z, core), col: 4 (over x), feat: 2 (over y_lo).
Axes of the slice: x: 4, y: 4 (y_hi: 2, y_lo: 2; y = y_hi * 2 + y_lo), z: 4, core: 2. Of those that a mesh axis runs over, the one named last changes fastest.
Arguments:
- block_values: float32 [16, 4, 240, 128, 128], P('row', 'col'), may hold values from -0.09375 to 0.09375
- block_rows: int32 [16, 4, 240], P('row', 'col'), may hold values from 0 to 15, as said below
- block_cols: int32 [16, 4, 240], P('row', 'col'), may hold values from 0 to 63, as said below
- block_count: int32 [16, 4], P('row', 'col'), may hold values from 1 to 240, as said below
- features: float32 [32768, 512], P(('col', 'row'), 'feat'), may hold values from -6 to 6
- weight: float32 [512, 512], P('feat'), may hold values from -0.25 to 0.25
- out_bias: float32 [512], replicated, may hold values from -3 to 3
- cotangent: float32 [32768, 512], P(('row', 'col', 'feat')), may hold values from -6 to 6
Outputs:
- activated: float32 [32768, 512], P(('row', 'col', 'feat'))
- grad_features: float32 [32768, 512], P(('col', 'row'), 'feat')
- grad_weight: float32 [512, 512], P('feat')
The draws below stay inside these ranges and needn't reach their ends.
Inputs may be any that keep to these rules, and one draw needn't show every extreme that they name: `block_rows`: slots below a tile's count name distinct blocks of that tile. `block_cols`: slots below a tile's count name distinct blocks of that tile. `block_count`: some tile uses all 240 slots; counts differ widely between tiles.
All inputs are finite; a program needn't handle non-finite values.
Results may differ from the reference program's by a relative error of at most 0.0003.
Values sent between devices are 32-bit elements; how exact they have to be, the bound alone decides.
No kernel may reach another device: no remote copies, remote signals or barrier semaphores. Data moves between devices by JAX's collectives and lax.ppermute only.
A program may use at most 192 MiB of HBM per device.

```python
import jax
import jax.numpy as jnp
from jax import lax

BLOCK = 128
F = 512
FO = 512
BR = 16
KMAX = 240
CB = 64
NODES = 32768
N_ROW = 16
N_COL = 4


def shared_layout(key):
    tile_keys = jax.random.split(key, N_ROW * N_COL)

    def one_tile(tile_key):
        return jax.random.permutation(tile_key, BR * CB)[:KMAX]
    picks = jax.vmap(one_tile)(tile_keys)
    return picks.reshape(N_ROW, N_COL, KMAX).astype(jnp.int32)


def draw_block_rows(key, part):
    layout = shared_layout(key)
    return layout // CB


def draw_block_cols(key, part):
    layout = shared_layout(key)
    return layout % CB


def draw_block_count(key, part):
    key = jax.random.fold_in(key, 7)
    level_key, cut_key, pick_key = jax.random.split(key, 3)
    levels = jax.random.randint(level_key, (N_ROW * N_COL,), 0, 4)
    based = jnp.right_shift(jnp.full((N_ROW * N_COL,), KMAX, jnp.int32), levels.astype(jnp.int32))
    cuts = jax.random.randint(cut_key, (N_ROW * N_COL,), 0, KMAX // 16 + 1).astype(jnp.int32)
    counts = jnp.maximum(based - cuts, 1)
    chosen = jax.random.randint(pick_key, (), 0, N_ROW * N_COL)
    counts = jnp.where(jnp.arange(N_ROW * N_COL) == chosen, KMAX, counts)
    return counts.reshape(N_ROW, N_COL).astype(jnp.int32)


def block_levels(rng, extent, pieces, least, top_value):
    gain, own = 1.0, jax.random.fold_in(rng, 6)
    for dim, shards_of in pieces:
        heights = jnp.exp(jax.random.uniform(jax.random.fold_in(own, dim), (shards_of,), jnp.float32, least / len(pieces), top_value / len(pieces)))
        gain = gain * jnp.repeat(heights, extent[dim] // shards_of).reshape([-1 if axis == dim else 1 for axis in range(len(extent))])
    return gain


def bell_draw(stream_key, dims, deviation, most, shards=(), held_as=jnp.bfloat16):
    result = jax.random.normal(stream_key, dims, jnp.float32) * deviation
    if len(shards) > 0:
        result = block_levels(stream_key, dims, shards, -0.22, 0.18) * result
    return jnp.clip(result, min=-most, max=most).astype(held_as)


def setup_inputs(seed: int = 0) -> dict:
    splits = jax.random.split(jax.random.key(seed), 9)
    block_values = bell_draw(splits[0], (N_ROW, N_COL, KMAX, BLOCK, BLOCK), (BLOCK * KMAX * N_COL // (2 * BR)) ** -0.5, 0.09375, ((0, 16), (1, 4)), jnp.float32)
    block_rows = draw_block_rows(jax.random.fold_in(splits[8], 71), 0)
    block_cols = draw_block_cols(jax.random.fold_in(splits[8], 71), 0)
    block_count = draw_block_count(jax.random.fold_in(splits[8], 71), 0)
    features = bell_draw(splits[4], (NODES, F), 1.0, 6.0, ((0, 64), (1, 2)), jnp.float32)
    weight = bell_draw(splits[5], (F, FO), F ** -0.5, 0.25, ((0, 2),), jnp.float32)
    out_bias = bell_draw(splits[6], (FO,), 0.5, 3.0, (), jnp.float32)
    cotangent = bell_draw(splits[7], (NODES, FO), 1.0, 6.0, ((0, 128),), jnp.float32)
    return {"block_values": block_values, "block_rows": block_rows, "block_cols": block_cols, "block_count": block_count, "features": features, "weight": weight, "out_bias": out_bias, "cotangent": cotangent}


HIGHEST_MODE = lax.Precision.HIGHEST


def forward_tile(values, tile_rows, tile_cols, slot_count, source, out_blocks):
    block_size = values.shape[1]
    feat_width = source.shape[1]
    picked = source.reshape(-1, block_size, feat_width)[tile_cols]
    products = jnp.einsum("kij,kjf->kif", values, picked, precision=HIGHEST_MODE)
    live_slots = (jnp.arange(values.shape[0], dtype=jnp.int32) < slot_count).astype(jnp.float32)
    onehot = (tile_rows[None, :] == jnp.arange(out_blocks, dtype=jnp.int32)[:, None]).astype(jnp.float32) * live_slots[None, :]
    summed = jnp.einsum("bk,kif->bif", onehot, products, precision=HIGHEST_MODE)
    return summed.reshape(out_blocks * block_size, feat_width)


def backward_tile(values, tile_rows, tile_cols, slot_count, source, out_blocks):
    block_size = values.shape[1]
    feat_width = source.shape[1]
    picked = source.reshape(-1, block_size, feat_width)[tile_rows]
    products = jnp.einsum("kji,kjf->kif", values, picked, precision=HIGHEST_MODE)
    live_slots = (jnp.arange(values.shape[0], dtype=jnp.int32) < slot_count).astype(jnp.float32)
    onehot = (tile_cols[None, :] == jnp.arange(out_blocks, dtype=jnp.int32)[:, None]).astype(jnp.float32) * live_slots[None, :]
    summed = jnp.einsum("ck,kif->cif", onehot, products, precision=HIGHEST_MODE)
    return summed.reshape(out_blocks * block_size, feat_width)


def reference(block_values, block_rows, block_cols, block_count, features, weight, out_bias, cotangent):
    column_feats = features.reshape(N_COL, CB * BLOCK, F)

    def row_total(row_index):
        def add_tile(totals, col_index):
            term = forward_tile(block_values[row_index, col_index], block_rows[row_index, col_index],
                                block_cols[row_index, col_index], block_count[row_index, col_index],
                                column_feats[col_index], BR)
            return totals + term, None

        totals, unused = lax.scan(add_tile, jnp.zeros((BR * BLOCK, F), jnp.float32),
                                  jnp.arange(N_COL, dtype=jnp.int32))
        return totals

    aggregated = lax.map(row_total, jnp.arange(N_ROW, dtype=jnp.int32)).reshape(NODES, F)
    pre_act = jnp.dot(aggregated, weight, precision=HIGHEST_MODE) + out_bias
    sigmoid_pre = jax.nn.sigmoid(pre_act)
    activated = pre_act * sigmoid_pre
    slope = cotangent * (sigmoid_pre * (1.0 + pre_act * (1.0 - sigmoid_pre)))
    grad_weight = jnp.einsum("nf,no->fo", aggregated, slope, precision=HIGHEST_MODE)
    back_rows = jnp.einsum("no,fo->nf", slope, weight, precision=HIGHEST_MODE).reshape(N_ROW, BR * BLOCK, F)

    def col_total(col_index):
        def add_tile(totals, row_index):
            term = backward_tile(block_values[row_index, col_index], block_rows[row_index, col_index],
                                 block_cols[row_index, col_index], block_count[row_index, col_index],
                                 back_rows[row_index], CB)
            return totals + term, None

        totals, unused = lax.scan(add_tile, jnp.zeros((CB * BLOCK, F), jnp.float32),
                                  jnp.arange(N_ROW, dtype=jnp.int32))
        return totals

    grad_features = lax.map(col_total, jnp.arange(N_COL, dtype=jnp.int32)).reshape(NODES, F)
    return activated, grad_features, grad_weight
```

```python
import functools

import jax
import jax.numpy as jnp
from jax import lax
from jax.experimental import pallas as pl
from jax.experimental.pallas import tpu as pltpu
from jax.sharding import PartitionSpec as P

BLK = 128
HIGH = lax.Precision.HIGH

Y, Z, C = 2, 4, 2


def row_perm(dy, dz, dc):
    pairs = []
    for y in range(Y):
        for z in range(Z):
            for c in range(C):
                there = ((y + dy) % Y) * 8 + ((z + dz) % Z) * 2 + (c + dc) % C
                pairs.append((y * 8 + z * 2 + c, there))
    return pairs


Z_UP, Z_DOWN = row_perm(0, 1, 0), row_perm(0, -1, 0)
Y_SWAP, CORE_SWAP = row_perm(1, 0, 0), row_perm(0, 0, 1)
X_UP = [(i, (i + 1) % 4) for i in range(4)]
X_DOWN = [(i, (i - 1) % 4) for i in range(4)]
F_SWAP = [(0, 1), (1, 0)]


def up_z(v):
    return lax.ppermute(v, "row", Z_UP)


def down_z(v):
    return lax.ppermute(v, "row", Z_DOWN)


def swap_y(v):
    return lax.ppermute(v, "row", Y_SWAP)


def swap_core(v):
    return lax.ppermute(v, "row", CORE_SWAP)


def up_x(v):
    return lax.ppermute(v, "col", X_UP)


def down_x(v):
    return lax.ppermute(v, "col", X_DOWN)


def swap_f(v):
    return lax.ppermute(v, "feat", F_SWAP)


def cat(*parts):
    return jnp.concatenate(parts, axis=0)


def split(v):
    hi = v.astype(jnp.bfloat16)
    lo = (v - hi.astype(jnp.float32)).astype(jnp.bfloat16)
    return hi, lo


def tile_kernel(steps, per_step, unroll, transpose, places, targets, n_src, *refs):
    src, dst, cnt, a_ref = refs[:4]
    x_refs = refs[4 : 4 + len(places)]
    o_refs = refs[4 + len(places) : 4 + len(places) + len(targets)]
    xcat, acc = refs[4 + len(places) + len(targets) :]
    step = pl.program_id(0)

    @pl.when(step == 0)
    def _():
        acc[...] = jnp.zeros_like(acc)
        for x_ref, spans in zip(x_refs, places):
            for first, at, n in spans:

                def convert(i, carry, x_ref=x_ref, first=first, at=at):
                    hi, lo = split(x_ref[first + i])
                    xcat[at + i, 0:128, :] = hi
                    xcat[at + i, 128:256, :] = hi
                    xcat[at + i, 256:384, :] = lo
                    return carry

                lax.fori_loop(0, n, convert, 0, unroll=min(n, 4))

    count = cnt[0]
    base = step * per_step
    here = jnp.clip(count - base, 0, per_step)

    def group(g, carry):
        for u in range(unroll):
            slot = g * unroll + u
            live = base + slot < count
            r = jnp.where(live, dst[base + slot], 0)
            c = jnp.where(live, src[base + slot], 0)
            a = jnp.where(live, a_ref[slot], 0.0)
            if transpose:
                a = a.T
            hi, lo = split(a)
            lhs = jnp.concatenate([hi, lo, hi], axis=1)
            acc[r] = acc[r] + jnp.dot(lhs, xcat[c], preferred_element_type=jnp.float32)
        return carry

    lax.fori_loop(0, lax.div(here + unroll - 1, unroll), group, 0)

    @pl.when(step == steps - 1)
    def _():
        for o_ref, (first, n) in zip(o_refs, targets):
            o_ref[...] = acc[first : first + n]


def tile_product(values, src, dst, cnt, pieces, places, targets, n_src, n_dst, transpose):
    slots = values.shape[0]
    per_step, unroll = 48, 16
    steps = slots // per_step
    width = pieces[0].shape[-1]
    pieces = [p.reshape(-1, BLK, width) for p in pieces]

    def whole(shape):
        return pl.BlockSpec(shape, lambda i, *_: (0, 0, 0), pipeline_mode=pl.Buffered(1))

    return pl.pallas_call(
        functools.partial(tile_kernel, steps, per_step, unroll, transpose, places, targets, n_src),
        grid_spec=pltpu.PrefetchScalarGridSpec(
            num_scalar_prefetch=3,
            grid=(steps,),
            in_specs=[pl.BlockSpec((per_step, BLK, BLK), lambda i, *_: (i, 0, 0))]
            + [whole(p.shape) for p in pieces],
            out_specs=[whole((n, BLK, width)) for _, n in targets],
            scratch_shapes=[
                pltpu.VMEM((n_src, 3 * BLK, width), jnp.bfloat16),
                pltpu.VMEM((n_dst, BLK, width), jnp.float32),
            ],
        ),
        out_shape=[jax.ShapeDtypeStruct((n, BLK, width), jnp.float32) for _, n in targets],
        compiler_params=pltpu.CompilerParams(vmem_limit_bytes=60 << 20),
        cost_estimate=pl.CostEstimate(
            flops=2 * slots * BLK * 3 * BLK * width,
            bytes_accessed=slots * BLK * BLK * 4 + (n_src + n_dst) * BLK * width * 4,
            transcendentals=0,
        ),
    )(src, dst, cnt, values, *pieces)


def gather_rows(shard):
    half = 256
    first, second = shard[:half], shard[half:]
    other = swap_y(shard)
    pair = cat(first, other[:half])
    a1, b1 = up_z(pair), down_z(pair)
    a2, b2 = up_z(second), down_z(second)
    c2_lo, c2_hi = up_z(a2[: half // 2]), down_z(b2[half // 2 :])
    c1_lo, c1_hi = up_z(a1[:half]), down_z(b1[half:])
    ya2, yb2 = swap_y(a2), swap_y(b2)
    yc2 = swap_y(cat(c2_lo, c2_hi))
    near = [shard, other, a1, b1, a2, b2, c1_lo, c1_hi, c2_lo, c2_hi, ya2, yb2, yc2]

    def at(dy, dz, blk):
        return dy * 16 + dz * 4 + blk

    spans = [
        [(0, at(0, 0, 0), 4)],
        [(0, at(1, 0, 0), 4)],
        [(0, at(0, 3, 0), 2), (2, at(1, 3, 0), 2)],
        [(0, at(0, 1, 0), 2), (2, at(1, 1, 0), 2)],
        [(0, at(0, 3, 2), 2)],
        [(0, at(0, 1, 2), 2)],
        [(0, at(0, 2, 0), 2)],
        [(0, at(1, 2, 0), 2)],
        [(0, at(0, 2, 2), 1)],
        [(0, at(0, 2, 3), 1)],
        [(0, at(1, 3, 2), 2)],
        [(0, at(1, 1, 2), 2)],
        [(0, at(1, 2, 2), 2)],
    ]
    far = [swap_core(p) for p in near]
    far_spans = [[(f, p + 32, n) for f, p, n in s] for s in spans]
    return near + far, spans + far_spans


def scatter_z(pieces, up, down):
    half = pieces[2].shape[0] // 2
    from_down = up(pieces[2][:half])
    from_up = down(pieces[2][half:])
    plus = up(cat(pieces[1][:half] + from_down, pieces[1][half:]))
    minus = down(cat(pieces[3][:half], pieces[3][half:] + from_up))
    return pieces[0] + plus + minus


def gather_ring(piece, up, down):
    half = piece.shape[0] // 2
    behind, ahead = up(piece), down(piece)
    lo, hi = up(behind[:half]), down(ahead[half:])
    return [piece, ahead, lo, hi, behind]


def weight_sum(part):
    core = lax.axis_index("row") % 2
    rows = part.shape[0] // 2
    mine = lax.dynamic_slice_in_dim(part, core * rows, rows)
    theirs = lax.dynamic_slice_in_dim(part, (1 - core) * rows, rows)
    mine = mine + swap_core(theirs)

    def scatter(v, axis, at, up, down, two):
        n = v.shape[0] // 4
        pick = [lax.dynamic_slice_in_dim(v, ((at + d) % 4) * n, n) for d in range(4)]
        return pick[0] + up(pick[1]) + down(pick[3]) + two(pick[2])

    def collect(v, at, up, down, two):
        n = v.shape[0]
        out = jnp.zeros((4 * n, v.shape[1]), v.dtype)
        for d, p in ((0, v), (3, up(v)), (1, down(v)), (2, two(v))):
            out = lax.dynamic_update_slice_in_dim(out, p, ((at + d) % 4) * n, 0)
        return out

    def two_z(v):
        return lax.ppermute(v, "row", row_perm(0, 2, 0))

    def two_x(v):
        return lax.ppermute(v, "col", [(i, (i + 2) % 4) for i in range(4)])

    z = (lax.axis_index("row") // 2) % 4
    x = lax.axis_index("col")
    mine = scatter(mine, "row", z, up_z, down_z, two_z)
    mine = scatter(mine, "col", x, up_x, down_x, two_x)
    mine = mine + swap_y(mine)
    mine = collect(mine, x, up_x, down_x, two_x)
    mine = collect(mine, z, up_z, down_z, two_z)
    theirs = swap_core(mine)
    return jnp.where(core == 0, cat(mine, theirs), cat(theirs, mine))


def on_device(
    block_values, block_rows, block_cols, block_count, features, weight, out_bias, cotangent
):
    values = block_values[0, 0]
    count = block_count[0]
    row, x, f = lax.axis_index("row"), lax.axis_index("col"), lax.axis_index("feat")
    y, z, core = row // 8, (row // 2) % 4, row % 2

    cols = jnp.clip(block_cols[0, 0], 0, 63)
    owner = cols // 4
    col_at = (
        ((owner % 2) ^ core) * 32
        + ((owner // 8) ^ y) * 16
        + (((owner // 2) - z) & 3) * 4
        + cols % 4
    ).astype(jnp.int32)
    rows = jnp.clip(block_rows[0, 0], 0, 15)
    row_at = ((((rows // 4) - x) & 3) * 4 + (((rows // 2) % 2) ^ f) * 2 + rows % 2).astype(
        jnp.int32
    )

    other_weight = swap_f(weight)

    with jax.named_scope("gather_features"):
        pieces, places = gather_rows(features)
    with jax.named_scope("aggregate"):
        own, ahead, across, behind = tile_product(
            values, col_at, row_at, count, pieces, places,
            ((0, 4), (4, 4), (8, 4), (12, 4)), 64, 16, False,
        )
    with jax.named_scope("sum_over_col"):
        parts = [v.reshape(512, 256) for v in (own, ahead, across, behind)]
        agg = scatter_z(parts, up_x, down_x)
    with jax.named_scope("activate"):
        agg_own, agg_other = agg[:256], swap_f(agg[256:])
        pre_act = (
            jnp.dot(agg_own, weight, precision=HIGH)
            + jnp.dot(agg_other, other_weight, precision=HIGH)
            + out_bias
        )
        sigmoid_pre = jax.nn.sigmoid(pre_act)
        activated = pre_act * sigmoid_pre
        slope = cotangent * (sigmoid_pre * (1.0 + pre_act * (1.0 - sigmoid_pre)))
        back_own = jnp.einsum("no,fo->nf", slope, weight, precision=HIGH)
        back_other = jnp.einsum("no,fo->nf", slope, other_weight, precision=HIGH)
        back = cat(back_own, swap_f(back_other))
    with jax.named_scope("gather_back"):
        ring = gather_ring(back, up_x, down_x)
    with jax.named_scope("back_tile"):
        back_places = [
            [(0, 0, 4)], [(0, 4, 4)], [(0, 8, 2)], [(0, 10, 2)], [(0, 12, 4)],
        ]
        near, far = tile_product(
            values, row_at, col_at, count, ring, back_places,
            ((0, 32), (32, 32)), 16, 64, True,
        )
    with jax.named_scope("weight_gradient"):
        part = jnp.einsum("nf,no->fo", agg_own, slope, precision=HIGH)
        part_other = jnp.einsum("nf,no->fo", agg_other, slope, precision=HIGH)
        grad_weight = weight_sum(part + swap_f(part_other))
    with jax.named_scope("sum_over_row"):
        near = near.reshape(2, 4, 512, 256)
        far = far.reshape(2, 4, 512, 256)
        far_two = swap_core(far[1, :, 256:])
        across_y = swap_y(near[1, :, 256:] + far_two)
        two = near[0, :, 256:] + swap_core(far[0, :, 256:]) + across_y
        two = scatter_z([two[d] for d in range(4)], up_z, down_z)
        one = near[:, :, :256] + swap_core(far[:, :, :256])
        one = scatter_z([cat(one[0, d], one[1, d]) for d in range(4)], up_z, down_z)
        one = one[:256] + swap_y(one[256:])
        grad_features = cat(one, two)
    return activated, grad_features, grad_weight


def solution(mesh):
    return jax.shard_map(
        on_device,
        mesh=mesh,
        in_specs=(
            P("row", "col", None, None, None),
            P("row", "col", None),
            P("row", "col", None),
            P("row", "col"),
            P(("col", "row"), "feat"),
            P("feat", None),
            P(),
            P(("row", "col", "feat"), None),
        ),
        out_specs=(P(("row", "col", "feat"), None), P(("col", "row"), "feat"), P("feat", None)),
        check_vma=False,
    )
```

```python
import functools

import jax
import jax.numpy as jnp
from jax import lax
from jax.experimental import pallas as pl
from jax.experimental.pallas import tpu as pltpu
from jax.sharding import PartitionSpec as P

BLK = 128
PER_STEP = 48
HIGH = lax.Precision.HIGH

Y, Z, C = 2, 4, 2


def row_perm(dy, dz, dc):
    pairs = []
    for y in range(Y):
        for z in range(Z):
            for c in range(C):
                there = ((y + dy) % Y) * 8 + ((z + dz) % Z) * 2 + (c + dc) % C
                pairs.append((y * 8 + z * 2 + c, there))
    return pairs


def move_z(v, dz):
    return lax.ppermute(v, "row", row_perm(0, dz, 0))


def swap_y(v):
    return lax.ppermute(v, "row", row_perm(1, 0, 0))


def swap_core(v):
    return lax.ppermute(v, "row", row_perm(0, 0, 1))


def move_x(v, dx):
    return lax.ppermute(v, "col", [(x, (x + dx) % 4) for x in range(4)])


def swap_f(v):
    return lax.ppermute(v, "feat", [(0, 1), (1, 0)])


def cat(*parts):
    return jnp.concatenate(parts, axis=0)


def by_place(parts, first):
    n = len(parts)
    rolled = cat(*parts, *parts[:-1]).reshape(2 * n - 1, *parts[0].shape)
    rolled = lax.dynamic_slice_in_dim(rolled, (n - first) % n, n)
    return rolled.reshape(n * parts[0].shape[0], *parts[0].shape[1:])


def split(v):
    hi = v.astype(jnp.bfloat16)
    lo = (v - hi.astype(jnp.float32)).astype(jnp.bfloat16)
    return hi, lo


def order_slots(group, live):
    key = jnp.where(live, group, 2).reshape(-1, PER_STEP).astype(jnp.int32)
    place = jnp.arange(PER_STEP, dtype=jnp.int32)
    before = (key[:, None, :] < key[:, :, None]) | (
        (key[:, None, :] == key[:, :, None]) & (place[None, None, :] < place[None, :, None])
    )
    rank = jnp.sum(before, axis=2, dtype=jnp.int32)
    order = jnp.sum(
        jnp.where(rank[:, None, :] == place[None, :, None], place[None, None, :], 0),
        axis=2,
        dtype=jnp.int32,
    )
    zero = jnp.zeros(key.shape[0], jnp.int32)
    first = jnp.sum(key == 0, axis=1, dtype=jnp.int32)
    both = jnp.sum(key <= 1, axis=1, dtype=jnp.int32)
    return order.reshape(-1), jnp.concatenate([zero, first, both])


def tile_kernel(steps, unroll, transpose, places, targets, bounds_at, carried, *refs):
    src, dst, order, bounds, a_ref = refs[:5]
    x_refs = refs[5 : 5 + len(places)]
    init = refs[5 + len(places)] if carried else None
    at = 5 + len(places) + int(carried)
    o_refs = refs[at : at + len(targets)]
    xcat, acc, sems = refs[at + len(targets) :]
    step = pl.program_id(0)

    @pl.when(step == 0)
    def _():
        if carried:
            acc[...] = init[...]
        else:
            acc[...] = jnp.zeros_like(acc)
        for x_ref, spans in zip(x_refs, places):
            for first, to, n in spans:

                def convert(i, carry, x_ref=x_ref, first=first, to=to):
                    hi, lo = split(x_ref[first + i])
                    xcat[to + i, 0:128, :] = hi
                    xcat[to + i, 128:256, :] = hi
                    xcat[to + i, 256:384, :] = lo
                    return carry

                lax.fori_loop(0, n, convert, 0, unroll=min(n, 4))

    begin = bounds[bounds_at * steps + step]
    end = bounds[(bounds_at + 1) * steps + step]
    base = step * PER_STEP

    def group(g, carry):
        for u in range(unroll):
            p = begin + g * unroll + u
            live = p < end
            slot = order[base + jnp.minimum(p, PER_STEP - 1)]
            r = jnp.where(live, dst[base + slot], 0)
            c = jnp.where(live, src[base + slot], 0)
            a = jnp.where(live, a_ref[slot], 0.0)
            if transpose:
                a = a.T
            hi, lo = split(a)
            lhs = jnp.concatenate([hi, lo, hi], axis=1)
            acc[r] = acc[r] + jnp.dot(lhs, xcat[c], preferred_element_type=jnp.float32)
        return carry

    lax.fori_loop(0, lax.div(end - begin + unroll - 1, unroll), group, 0)

    @pl.when(step == steps - 1)
    def _():
        copies = [
            pltpu.make_async_copy(acc.at[pl.ds(first, n)], o_ref, sems.at[i])
            for i, (o_ref, (first, n)) in enumerate(zip(o_refs, targets))
        ]
        for copy in copies:
            copy.start()
        for copy in copies:
            copy.wait()


def tile_product(values, src, dst, plan, part, pieces, places, targets, transpose, unroll, limit, init=None):
    order, bounds = plan
    slots = values.shape[0]
    steps = slots // PER_STEP
    width = pieces[0].shape[-1]
    pieces = [p.reshape(-1, BLK, width) for p in pieces]
    n_src = max(to + n for spans in places for _, to, n in spans)
    n_dst = max(first + n for first, n in targets)
    inits = [] if init is None else [init]

    def whole(shape):
        return pl.BlockSpec(shape, lambda i, *_: (0, 0, 0), pipeline_mode=pl.Buffered(1))

    return pl.pallas_call(
        functools.partial(
            tile_kernel, steps, unroll, transpose, places, targets, part, init is not None
        ),
        grid_spec=pltpu.PrefetchScalarGridSpec(
            num_scalar_prefetch=4,
            grid=(steps,),
            in_specs=[pl.BlockSpec((PER_STEP, BLK, BLK), lambda i, *_: (i, 0, 0))]
            + [whole(p.shape) for p in pieces + inits],
            out_specs=[pl.BlockSpec(memory_space=pl.ANY) for _ in targets],
            scratch_shapes=[
                pltpu.VMEM((n_src, 3 * BLK, width), jnp.bfloat16),
                pltpu.VMEM((n_dst, BLK, width), jnp.float32),
                pltpu.SemaphoreType.DMA((len(targets),)),
            ],
        ),
        out_shape=[jax.ShapeDtypeStruct((n, BLK, width), jnp.float32) for _, n in targets],
        compiler_params=pltpu.CompilerParams(vmem_limit_bytes=limit << 20),
        cost_estimate=pl.CostEstimate(
            flops=slots * BLK * 3 * BLK * width,
            bytes_accessed=slots * BLK * BLK * 4 + (n_src + n_dst) * BLK * width * 4,
            transcendentals=0,
        ),
    )(src, dst, order, bounds, values, *pieces, *inits)


def on_device(
    block_values, block_rows, block_cols, block_count, features, weight, out_bias, cotangent
):
    values = block_values[0, 0]
    live = jnp.arange(values.shape[0], dtype=jnp.int32) < block_count[0, 0]
    row, x, f = lax.axis_index("row"), lax.axis_index("col"), lax.axis_index("feat")
    y, z, core = row // 8, (row // 2) % 4, row % 2

    cols = jnp.clip(block_cols[0, 0], 0, 63)
    rows = jnp.clip(block_rows[0, 0], 0, 15)
    owner = cols // 4
    dc, dy, dz, blk = (owner % 2) ^ core, (owner // 8) ^ y, ((owner // 2) - z) & 3, cols % 4
    dx, df = ((rows // 4) - x) & 3, ((rows // 2) % 2) ^ f
    row_at = dx * 4 + df * 2 + rows % 2

    early = (dz == 0) | ((dy == 0) & (blk >= 2))
    seq = jnp.where(dz == 3, 0, dz)
    col_early = dc * 14 + jnp.where(dz == 0, dy * 4 + blk, 8 + seq * 2 + blk - 2)
    col_late = dc * 18 + jnp.where(blk < 2, seq * 4 + dy * 2 + blk, 12 + seq * 2 + blk - 2)
    col_src = jnp.where(early, col_early, col_late)
    forward_plan = order_slots(jnp.where(early, 0, 1), live)

    col_dst = dc * 16 + jnp.where(blk >= 2, dy * 8 + dz * 2 + blk - 2, 32 + dz * 4 + dy * 2 + blk)
    backward_plan = order_slots(jnp.zeros_like(rows), live)

    half = 256
    with jax.named_scope("gather_features"):
        other = swap_y(features)
        second, forward_order = lax.optimization_barrier((features[half:], forward_plan[0]))
        forward_plan = (forward_order, forward_plan[1])
        z_two = cat(*[move_z(second, d) for d in (1, -1, 2)])
        y_two = swap_y(z_two)
        near_early = [features, other, z_two]
        far_early = [swap_core(v) for v in near_early]
        pair = cat(features[:half], other[:half])
        near_late = [move_z(pair, d) for d in (1, -1, 2)]
    with jax.named_scope("aggregate"):
        early_places = [[(0, at, n)] for at, n in ((0, 4), (4, 4), (8, 6))]
        early_places += [[(0, 14 + at, n)] for ((_, at, n),) in early_places]
        (early_sum,) = tile_product(
            values, col_src, row_at, forward_plan, 0, near_early + far_early, early_places,
            ((0, 16),), False, 8, 44,
        )
    with jax.named_scope("gather_features"):
        *near_late, y_two, early_sum = lax.optimization_barrier((*near_late, y_two, early_sum))
        near_late = near_late + [y_two]
        far_late = [swap_core(v) for v in near_late]
    with jax.named_scope("aggregate"):
        late_places = [[(0, at, n)] for at, n in ((0, 4), (4, 4), (8, 4), (12, 6))]
        late_places += [[(0, 18 + at, n)] for ((_, at, n),) in late_places]
        own, ahead, across, behind = tile_product(
            values, col_src, row_at, forward_plan, 1, near_late + far_late, late_places,
            ((0, 4), (4, 4), (8, 4), (12, 4)), False, 8, 44, early_sum,
        )
    with jax.named_scope("sum_over_col"):
        own, ahead, across, behind = [v.reshape(512, 256) for v in (own, ahead, across, behind)]
        weight_in, cotangent_in, own = lax.optimization_barrier((weight, cotangent, own))
        across, ahead, behind = move_x(across, 2), move_x(ahead, 1), move_x(behind, -1)
        other_weight, other_cotangent = swap_f(weight_in), swap_f(cotangent_in)
        agg = own + ahead + behind + across
        agg, other_weight, other_cotangent = lax.optimization_barrier(
            (agg, other_weight, other_cotangent)
        )
    with jax.named_scope("activate"):
        other_agg = swap_f(cat(agg[half:], agg[:half]))
        pre_act = (
            jnp.dot(agg, weight, precision=HIGH)
            + jnp.dot(other_agg, other_weight, precision=HIGH)
            + out_bias
        )
        sigmoid_pre = jax.nn.sigmoid(pre_act)
        activated = (pre_act * sigmoid_pre)[:half]
        both = cat(cotangent, other_cotangent)
        slope = both * (sigmoid_pre * (1.0 + pre_act * (1.0 - sigmoid_pre)))
        back = jnp.einsum("no,fo->nf", slope, weight, precision=HIGH)
    with jax.named_scope("gather_back"):
        ring = [back] + [move_x(back, -d) for d in (1, 2, 3)]
    with jax.named_scope("weight_gradient"):
        slope, agg, back = lax.optimization_barrier((slope, agg, back))
        gw = jnp.einsum("nf,no->fo", agg, slope, precision=HIGH)
        gw = lax.all_to_all(gw, ("row", "col"), 0, 0, tiled=True)
        gw = jnp.sum(gw.reshape(64, 4, 512), axis=0)
        gw, ring[0] = lax.optimization_barrier((gw, back))
    with jax.named_scope("back_tile"):
        near_two_0, near_two_1, far_two, near_one, far_one = tile_product(
            values, row_at, col_dst, backward_plan, 0, ring,
            [[(0, 4 * i, 4)] for i in range(4)],
            ((0, 8), (8, 8), (16, 16), (32, 16), (48, 16)), True, 16, 30,
        )
    with jax.named_scope("sum_over_row"):
        far_two = swap_core(far_two.reshape(2, 4, 256, 256))
        far_one = swap_core(far_one.reshape(4, 512, 256))
        two_1 = near_two_1.reshape(4, 256, 256) + far_two[1]
        near_one = near_one.reshape(4, 512, 256)
        one = [near_one[d] + far_one[d] for d in range(4)]
        *one, gw, two_1 = lax.optimization_barrier((*one, gw, two_1))
        two_1 = swap_y(two_1)
        one = one[0] + move_z(one[1], 1) + move_z(one[3], -1) + move_z(one[2], 2)
    with jax.named_scope("weight_gradient"):
        gw = jnp.broadcast_to(gw[None], (4, 4, 512)).reshape(16, 512)
        gw = lax.all_to_all(gw, "col", 0, 0, tiled=True)
        gw = jnp.broadcast_to(gw[None], (4, 16, 512)).reshape(64, 512)
        along_z = [[8 * i + 2 * j + k for j in range(4)] for i in range(2) for k in range(2)]
        gw = lax.all_to_all(gw, "row", 0, 0, tiled=True, axis_index_groups=along_z)
        gw, two_1 = lax.optimization_barrier((gw.reshape(128, 256), two_1))
    with jax.named_scope("sum_over_row"):
        two = two_1 + (near_two_0.reshape(4, 256, 256) + far_two[0])
        message, two = lax.optimization_barrier((cat(one[half:], gw), two))
        came = swap_y(message)
        two = two[0] + move_z(two[1], 1) + move_z(two[3], -1) + move_z(two[2], 2)
        grad_features = cat(one[:half] + came[:half], two)
    with jax.named_scope("weight_gradient"):
        gw = by_place([gw, came[half:]], y)
        grad_weight = by_place([gw, swap_core(gw)], core)
        grad_weight = grad_weight.reshape(2, 2, 4, 16, 512).transpose(1, 2, 0, 3, 4)
        grad_weight = grad_weight.reshape(256, 512)
    return activated, grad_features, grad_weight


def solution(mesh):
    return jax.shard_map(
        on_device,
        mesh=mesh,
        in_specs=(
            P("row", "col", None, None, None),
            P("row", "col", None),
            P("row", "col", None),
            P("row", "col"),
            P(("col", "row"), "feat"),
            P("feat", None),
            P(),
            P(("row", "col", "feat"), None),
        ),
        out_specs=(P(("row", "col", "feat"), None), P(("col", "row"), "feat"), P("feat", None)),
        check_vma=False,
    )
```

```python
import functools

import jax
import jax.numpy as jnp
from jax import lax
from jax.experimental import pallas as pl
from jax.experimental.pallas import tpu as pltpu
from jax.sharding import PartitionSpec as P

BLK = 128
PER_STEP = 48
HIGH = lax.Precision.HIGH

Y, Z, C = 2, 4, 2


def row_perm(dy, dz, dc):
    pairs = []
    for y in range(Y):
        for z in range(Z):
            for c in range(C):
                there = ((y + dy) % Y) * 8 + ((z + dz) % Z) * 2 + (c + dc) % C
                pairs.append((y * 8 + z * 2 + c, there))
    return pairs


def move_z(v, dz):
    return lax.ppermute(v, "row", row_perm(0, dz, 0))


def swap_y(v):
    return lax.ppermute(v, "row", row_perm(1, 0, 0))


def swap_core(v):
    return lax.ppermute(v, "row", row_perm(0, 0, 1))


def move_x(v, dx):
    return lax.ppermute(v, "col", [(x, (x + dx) % 4) for x in range(4)])


def swap_f(v):
    return lax.ppermute(v, "feat", [(0, 1), (1, 0)])


def cat(*parts):
    return jnp.concatenate(parts, axis=0)


def split(v):
    hi = v.astype(jnp.bfloat16)
    lo = (v - hi.astype(jnp.float32)).astype(jnp.bfloat16)
    return hi, lo


def order_slots(group, live):
    key = jnp.where(live, group, 2).reshape(-1, PER_STEP).astype(jnp.int32)
    place = jnp.arange(PER_STEP, dtype=jnp.int32)
    before = (key[:, None, :] < key[:, :, None]) | (
        (key[:, None, :] == key[:, :, None]) & (place[None, None, :] < place[None, :, None])
    )
    rank = jnp.sum(before, axis=2, dtype=jnp.int32)
    order = jnp.sum(
        jnp.where(rank[:, None, :] == place[None, :, None], place[None, None, :], 0),
        axis=2,
        dtype=jnp.int32,
    )
    zero = jnp.zeros(key.shape[0], jnp.int32)
    first = jnp.sum(key == 0, axis=1, dtype=jnp.int32)
    both = jnp.sum(key <= 1, axis=1, dtype=jnp.int32)
    return order.reshape(-1), jnp.concatenate([zero, first, both])


def tile_kernel(steps, transpose, places, targets, bounds_at, carried, *refs):
    src, dst, order, bounds, a_ref = refs[:5]
    x_refs = refs[5 : 5 + len(places)]
    init = refs[5 + len(places)] if carried else None
    at = 5 + len(places) + int(carried)
    o_refs = refs[at : at + len(targets)]
    xcat, acc, sems = refs[at + len(targets) :]
    step = pl.program_id(0)

    @pl.when(step == 0)
    def _():
        if carried:
            acc[...] = init[...]
        else:
            acc[...] = jnp.zeros_like(acc)
        for x_ref, spans in zip(x_refs, places):
            for first, to, n in spans:

                def convert(i, carry, x_ref=x_ref, first=first, to=to):
                    hi, lo = split(x_ref[first + i])
                    xcat[to + i, 0:128, :] = hi
                    xcat[to + i, 128:256, :] = hi
                    xcat[to + i, 256:384, :] = lo
                    return carry

                lax.fori_loop(0, n, convert, 0, unroll=min(n, 4))

    begin = bounds[bounds_at * steps + step]
    end = bounds[(bounds_at + 1) * steps + step]
    base = step * PER_STEP

    def group(first, size):
        for u in range(size):
            p = first + u
            live = p < end
            slot = order[base + jnp.minimum(p, PER_STEP - 1)]
            r = jnp.where(live, dst[base + slot], 0)
            c = jnp.where(live, src[base + slot], 0)
            a = jnp.where(live, a_ref[slot], 0.0)
            if transpose:
                a = a.T
            hi, lo = split(a)
            lhs = jnp.concatenate([hi, lo, hi], axis=1)
            acc[r] = acc[r] + jnp.dot(lhs, xcat[c], preferred_element_type=jnp.float32)

    full = lax.div(end - begin + 9, 16)
    rest = begin + full * 16

    def large(g, carry):
        group(begin + g * 16, 16)
        return carry

    def small(g, carry):
        group(rest + g * 4, 4)
        return carry

    lax.fori_loop(0, full, large, 0)
    lax.fori_loop(0, lax.div(jnp.maximum(end - rest, 0) + 3, 4), small, 0)

    @pl.when(step == steps - 1)
    def _():
        copies = [
            pltpu.make_async_copy(acc.at[pl.ds(first, n)], o_ref, sems.at[i])
            for i, (o_ref, (first, n)) in enumerate(zip(o_refs, targets))
        ]
        for copy in copies:
            copy.start()
        for copy in copies:
            copy.wait()


def tile_product(values, src, dst, plan, part, pieces, places, targets, transpose, limit, init=None):
    order, bounds = plan
    slots = values.shape[0]
    steps = slots // PER_STEP
    width = pieces[0].shape[-1]
    pieces = [p.reshape(-1, BLK, width) for p in pieces]
    n_src = max(to + n for spans in places for _, to, n in spans)
    n_dst = max(first + n for first, n in targets)
    inits = [] if init is None else [init]

    def whole(shape):
        return pl.BlockSpec(shape, lambda i, *_: (0, 0, 0), pipeline_mode=pl.Buffered(1))

    return pl.pallas_call(
        functools.partial(
            tile_kernel, steps, transpose, places, targets, part, init is not None
        ),
        grid_spec=pltpu.PrefetchScalarGridSpec(
            num_scalar_prefetch=4,
            grid=(steps,),
            in_specs=[pl.BlockSpec((PER_STEP, BLK, BLK), lambda i, *_: (i, 0, 0))]
            + [whole(p.shape) for p in pieces + inits],
            out_specs=[pl.BlockSpec(memory_space=pl.ANY) for _ in targets],
            scratch_shapes=[
                pltpu.VMEM((n_src, 3 * BLK, width), jnp.bfloat16),
                pltpu.VMEM((n_dst, BLK, width), jnp.float32),
                pltpu.SemaphoreType.DMA((len(targets),)),
            ],
        ),
        out_shape=[jax.ShapeDtypeStruct((n, BLK, width), jnp.float32) for _, n in targets],
        compiler_params=pltpu.CompilerParams(vmem_limit_bytes=limit << 20),
        cost_estimate=pl.CostEstimate(
            flops=slots * BLK * 3 * BLK * width,
            bytes_accessed=slots * BLK * BLK * 4 + (n_src + n_dst) * BLK * width * 4,
            transcendentals=0,
        ),
    )(src, dst, order, bounds, values, *pieces, *inits)


def on_device(
    block_values, block_rows, block_cols, block_count, features, weight, out_bias, cotangent
):
    values = block_values[0, 0]
    live = jnp.arange(values.shape[0], dtype=jnp.int32) < block_count[0, 0]
    row, x, f = lax.axis_index("row"), lax.axis_index("col"), lax.axis_index("feat")
    y, z, core = row // 8, (row // 2) % 4, row % 2

    cols = jnp.clip(block_cols[0, 0], 0, 63)
    rows = jnp.clip(block_rows[0, 0], 0, 15)
    owner = cols // 4
    dc, dy, dz, blk = (owner % 2) ^ core, (owner // 8) ^ y, ((owner // 2) - z) & 3, cols % 4
    dx, df = ((rows // 4) - x) & 3, ((rows // 2) % 2) ^ f
    row_at = dx * 4 + df * 2 + rows % 2

    early = (dz == 0) | ((dy == 0) & (blk >= 2)) | ((dz != 2) & (blk < 2))
    seq = jnp.where(dz == 3, 0, dz)
    col_early = dc * 22 + jnp.where(
        dz == 0, dy * 4 + blk, jnp.where(blk >= 2, 8 + seq * 2 + blk - 2, 14 + seq * 4 + dy * 2 + blk)
    )
    col_late = dc * 10 + jnp.where(blk >= 2, 4 + seq * 2 + blk - 2, dy * 2 + blk)
    col_src = jnp.where(early, col_early, col_late)
    forward_plan = order_slots(jnp.where(early, 0, 1), live)

    col_dst = dc * 16 + jnp.where(blk >= 2, dy * 8 + dz * 2 + blk - 2, 32 + dz * 4 + dy * 2 + blk)
    backward_plan = order_slots(jnp.zeros_like(rows), live)

    half = 256
    with jax.named_scope("gather_features"):
        other = swap_y(features)
        second, forward_order = lax.optimization_barrier((features[half:], forward_plan[0]))
        forward_plan = (forward_order, forward_plan[1])
        z_two = cat(*[move_z(second, d) for d in (1, -1, 2)])
        y_two = swap_y(z_two)
        pair = cat(features[:half], other[:half])
        below, above = move_z(pair, 1), move_z(pair, -1)
        near_early = [features, other, z_two, below, above]
        far_early = [swap_core(v) for v in near_early]
        across = [move_z(below[:half], 1), move_z(above[half:], -1)]
    with jax.named_scope("aggregate"):
        places = ((0, 4), (4, 4), (8, 6), (14, 4), (18, 4))
        places += tuple((22 + at, n) for at, n in places)
        (early_sum,) = tile_product(
            values, col_src, row_at, forward_plan, 0, near_early + far_early,
            [[(0, at, n)] for at, n in places], ((0, 16),), False, 44,
        )
    with jax.named_scope("gather_features"):
        *across, y_two, early_sum = lax.optimization_barrier((*across, y_two, early_sum))
        near_late = [cat(*across), y_two]
        far_late = [swap_core(v) for v in near_late]
    with jax.named_scope("aggregate"):
        places = ((0, 4), (4, 6), (10, 4), (14, 6))
        own, ahead, across, behind = tile_product(
            values, col_src, row_at, forward_plan, 1, near_late + far_late,
            [[(0, at, n)] for at, n in places],
            ((0, 4), (4, 4), (8, 4), (12, 4)), False, 44, early_sum,
        )
    with jax.named_scope("sum_over_col"):
        own, ahead, across, behind = [v.reshape(512, 256) for v in (own, ahead, across, behind)]
        weight_in, cotangent_in, own = lax.optimization_barrier((weight, cotangent, own))
        across, ahead, behind = move_x(across, 2), move_x(ahead, 1), move_x(behind, -1)
        other_weight, other_cotangent = swap_f(weight_in), swap_f(cotangent_in)
        agg = own + ahead + behind + across
        agg, other_weight, other_cotangent = lax.optimization_barrier(
            (agg, other_weight, other_cotangent)
        )
    with jax.named_scope("activate"):
        other_agg = swap_f(cat(agg[half:], agg[:half]))
        pre_act = (
            jnp.dot(agg, weight, precision=HIGH)
            + jnp.dot(other_agg, other_weight, precision=HIGH)
            + out_bias
        )
        sigmoid_pre = jax.nn.sigmoid(pre_act)
        activated = (pre_act * sigmoid_pre)[:half]
        both = cat(cotangent, other_cotangent)
        slope = both * (sigmoid_pre * (1.0 + pre_act * (1.0 - sigmoid_pre)))
        back = jnp.einsum("no,fo->nf", slope, weight, precision=HIGH)
    with jax.named_scope("gather_back"):
        ring = [back] + [move_x(back, -d) for d in (1, 2, 3)]
    with jax.named_scope("weight_gradient"):
        slope, agg, back = lax.optimization_barrier((slope, agg, back))
        gw = jnp.einsum("nf,no->fo", agg, slope, precision=HIGH)
        gw = lax.all_to_all(gw, "row", 0, 0, tiled=True)
        gw = jnp.sum(gw.reshape(16, 16, 512), axis=0)
        gw, ring[0] = lax.optimization_barrier((gw, back))
    with jax.named_scope("back_tile"):
        near_two_0, near_two_1, far_two_0, far_two_1, near_one, far_one = tile_product(
            values, row_at, col_dst, backward_plan, 0, ring,
            [[(0, 4 * i, 4)] for i in range(4)],
            ((0, 8), (8, 8), (16, 8), (24, 8), (32, 16), (48, 16)), True, 30,
        )
    with jax.named_scope("sum_over_row"):
        far_two_1 = swap_core(far_two_1.reshape(4, 256, 256))
        far_one = swap_core(far_one.reshape(4, 512, 256))
        far_two_0 = swap_core(far_two_0.reshape(4, 256, 256))
        two_1 = near_two_1.reshape(4, 256, 256) + far_two_1
        near_one, two_sum = lax.optimization_barrier((near_one.reshape(4, 512, 256), two_1))
        one = [near_one[d] + far_one[d] for d in range(4)]
        gw, *one = lax.optimization_barrier((gw, *one))
        two_1 = swap_y(two_sum)
        one = [one[0], move_z(one[1], 1), move_z(one[3], -1), move_z(one[2], 2)]
    with jax.named_scope("weight_gradient"):
        gw = jnp.broadcast_to(gw[None], (4, 16, 512)).reshape(64, 512)
        gw = lax.all_to_all(gw, "col", 0, 0, tiled=True)
        gw = jnp.sum(gw.reshape(4, 16, 512), axis=0)
        gw = jnp.broadcast_to(gw[None], (16, 16, 512)).reshape(256, 512)
        grad_weight = lax.all_to_all(gw, "row", 0, 0, tiled=True)
        grad_weight, two_1 = lax.optimization_barrier((grad_weight, two_1))
    with jax.named_scope("sum_over_row"):
        two = two_1 + (near_two_0.reshape(4, 256, 256) + far_two_0)
        one = one[0] + one[1] + one[2] + one[3]
        one, two = lax.optimization_barrier((one, two))
        two = two[0] + move_z(two[1], 1) + move_z(two[3], -1) + move_z(two[2], 2)
        grad_features = cat(one[:half] + swap_y(one[half:]), two)
    return activated, grad_features, grad_weight


def solution(mesh):
    return jax.shard_map(
        on_device,
        mesh=mesh,
        in_specs=(
            P("row", "col", None, None, None),
            P("row", "col", None),
            P("row", "col", None),
            P("row", "col"),
            P(("col", "row"), "feat"),
            P("feat", None),
            P(),
            P(("row", "col", "feat"), None),
        ),
        out_specs=(P(("row", "col", "feat"), None), P(("col", "row"), "feat"), P("feat", None)),
        check_vma=False,
    )
```

```python
import functools

import jax
import jax.numpy as jnp
from jax import lax
from jax.experimental import pallas as pl
from jax.experimental.pallas import tpu as pltpu
from jax.sharding import PartitionSpec as P

BLK = 128
PER_STEP = 48
HIGH = lax.Precision.HIGH

Y, Z, C = 2, 4, 2


def row_perm(dy, dz, dc):
    pairs = []
    for y in range(Y):
        for z in range(Z):
            for c in range(C):
                there = ((y + dy) % Y) * 8 + ((z + dz) % Z) * 2 + (c + dc) % C
                pairs.append((y * 8 + z * 2 + c, there))
    return pairs


def move_z(v, dz):
    return lax.ppermute(v, "row", row_perm(0, dz, 0))


def swap_y(v):
    return lax.ppermute(v, "row", row_perm(1, 0, 0))


def swap_core(v):
    return lax.ppermute(v, "row", row_perm(0, 0, 1))


def move_x(v, dx):
    return lax.ppermute(v, "col", [(x, (x + dx) % 4) for x in range(4)])


def swap_f(v):
    return lax.ppermute(v, "feat", [(0, 1), (1, 0)])


def cat(*parts):
    return jnp.concatenate(parts, axis=0)


def split(v):
    hi = v.astype(jnp.bfloat16)
    lo = (v - hi.astype(jnp.float32)).astype(jnp.bfloat16)
    return hi, lo


def order_slots(group, live):
    key = jnp.where(live, group, 2).reshape(-1, PER_STEP).astype(jnp.int32)
    place = jnp.arange(PER_STEP, dtype=jnp.int32)
    before = (key[:, None, :] < key[:, :, None]) | (
        (key[:, None, :] == key[:, :, None]) & (place[None, None, :] < place[None, :, None])
    )
    rank = jnp.sum(before, axis=2, dtype=jnp.int32)
    order = jnp.sum(
        jnp.where(rank[:, None, :] == place[None, :, None], place[None, None, :], 0),
        axis=2,
        dtype=jnp.int32,
    )
    zero = jnp.zeros(key.shape[0], jnp.int32)
    first = jnp.sum(key == 0, axis=1, dtype=jnp.int32)
    both = jnp.sum(key <= 1, axis=1, dtype=jnp.int32)
    return order.reshape(-1), jnp.concatenate([zero, first, both])


def tile_kernel(steps, transpose, places, targets, bounds_at, carried, *refs):
    src, dst, order, bounds, a_ref = refs[:5]
    x_refs = refs[5 : 5 + len(places)]
    init = refs[5 + len(places)] if carried else None
    at = 5 + len(places) + int(carried)
    o_refs = refs[at : at + len(targets)]
    xcat, acc, sems = refs[at + len(targets) :]
    step = pl.program_id(0)

    @pl.when(step == 0)
    def _():
        if carried:
            acc[...] = init[...]
        else:
            acc[...] = jnp.zeros_like(acc)
        for x_ref, spans in zip(x_refs, places):
            for first, to, n in spans:

                def convert(i, carry, x_ref=x_ref, first=first, to=to):
                    hi, lo = split(x_ref[first + i])
                    xcat[to + i, 0:128, :] = hi
                    xcat[to + i, 128:256, :] = hi
                    xcat[to + i, 256:384, :] = lo
                    return carry

                lax.fori_loop(0, n, convert, 0, unroll=min(n, 4))

    begin = bounds[bounds_at * steps + step]
    end = bounds[(bounds_at + 1) * steps + step]
    base = step * PER_STEP

    def group(first, size):
        for u in range(size):
            p = first + u
            live = p < end
            slot = order[base + jnp.minimum(p, PER_STEP - 1)]
            r = jnp.where(live, dst[base + slot], 0)
            c = jnp.where(live, src[base + slot], 0)
            a = jnp.where(live, a_ref[slot], 0.0)
            if transpose:
                a = a.T
            hi, lo = split(a)
            lhs = jnp.concatenate([hi, lo, hi], axis=1)
            acc[r] = acc[r] + jnp.dot(lhs, xcat[c], preferred_element_type=jnp.float32)

    full = lax.div(end - begin + 9, 16)
    rest = begin + full * 16

    def large(g, carry):
        group(begin + g * 16, 16)
        return carry

    def small(g, carry):
        group(rest + g * 4, 4)
        return carry

    lax.fori_loop(0, full, large, 0)
    lax.fori_loop(0, lax.div(jnp.maximum(end - rest, 0) + 3, 4), small, 0)

    @pl.when(step == steps - 1)
    def _():
        copies = [
            pltpu.make_async_copy(acc.at[pl.ds(first, n)], o_ref, sems.at[i])
            for i, (o_ref, (first, n)) in enumerate(zip(o_refs, targets))
        ]
        for copy in copies:
            copy.start()
        for copy in copies:
            copy.wait()


def tile_product(values, src, dst, plan, part, pieces, places, targets, transpose, limit, init=None):
    order, bounds = plan
    slots = values.shape[0]
    steps = slots // PER_STEP
    width = pieces[0].shape[-1]
    pieces = [p.reshape(-1, BLK, width) for p in pieces]
    n_src = max(to + n for spans in places for _, to, n in spans)
    n_dst = max(first + n for first, n in targets)
    inits = [] if init is None else [init]

    def whole(shape):
        return pl.BlockSpec(shape, lambda i, *_: (0, 0, 0), pipeline_mode=pl.Buffered(1))

    return pl.pallas_call(
        functools.partial(
            tile_kernel, steps, transpose, places, targets, part, init is not None
        ),
        grid_spec=pltpu.PrefetchScalarGridSpec(
            num_scalar_prefetch=4,
            grid=(steps,),
            in_specs=[pl.BlockSpec((PER_STEP, BLK, BLK), lambda i, *_: (i, 0, 0))]
            + [whole(p.shape) for p in pieces + inits],
            out_specs=[pl.BlockSpec(memory_space=pl.ANY) for _ in targets],
            scratch_shapes=[
                pltpu.VMEM((n_src, 3 * BLK, width), jnp.bfloat16),
                pltpu.VMEM((n_dst, BLK, width), jnp.float32),
                pltpu.SemaphoreType.DMA((len(targets),)),
            ],
        ),
        out_shape=[jax.ShapeDtypeStruct((n, BLK, width), jnp.float32) for _, n in targets],
        compiler_params=pltpu.CompilerParams(vmem_limit_bytes=limit << 20),
        cost_estimate=pl.CostEstimate(
            flops=slots * BLK * 3 * BLK * width,
            bytes_accessed=slots * BLK * BLK * 4 + (n_src + n_dst) * BLK * width * 4,
            transcendentals=0,
        ),
    )(src, dst, order, bounds, values, *pieces, *inits)


def on_device(
    block_values, block_rows, block_cols, block_count, features, weight, out_bias, cotangent
):
    values = block_values[0, 0]
    live = jnp.arange(values.shape[0], dtype=jnp.int32) < block_count[0, 0]
    row, x, f = lax.axis_index("row"), lax.axis_index("col"), lax.axis_index("feat")
    y, z, core = row // 8, (row // 2) % 4, row % 2

    cols = jnp.clip(block_cols[0, 0], 0, 63)
    rows = jnp.clip(block_rows[0, 0], 0, 15)
    owner = cols // 4
    dc, dy, dz, blk = (owner % 2) ^ core, (owner // 8) ^ y, ((owner // 2) - z) & 3, cols % 4
    dx, df = ((rows // 4) - x) & 3, ((rows // 2) % 2) ^ f
    row_at = dx * 4 + df * 2 + rows % 2

    early = (dz == 0) | ((dy == 0) & (blk >= 2)) | ((dz != 2) & (blk < 2))
    seq = jnp.where(dz == 3, 0, dz)
    col_early = dc * 22 + jnp.where(
        dz == 0, dy * 4 + blk, jnp.where(blk >= 2, 8 + seq * 2 + blk - 2, 14 + seq * 4 + dy * 2 + blk)
    )
    col_late = dc * 10 + jnp.where(blk >= 2, 4 + seq * 2 + blk - 2, dy * 2 + blk)
    col_src = jnp.where(early, col_early, col_late)
    forward_plan = order_slots(jnp.where(early, 0, 1), live)

    col_dst = dc * 16 + jnp.where(blk >= 2, dy * 8 + dz * 2 + blk - 2, 32 + dz * 4 + dy * 2 + blk)
    backward_plan = order_slots(jnp.zeros_like(rows), live)

    half = 256
    with jax.named_scope("gather_features"):
        other = swap_y(features)
        second, forward_order = lax.optimization_barrier((features[half:], forward_plan[0]))
        forward_plan = (forward_order, forward_plan[1])
        z_two = cat(*[move_z(second, d) for d in (1, -1, 2)])
        y_two = swap_y(z_two)
        pair = cat(features[:half], other[:half])
        below, above = move_z(pair, 1), move_z(pair, -1)
        near_early = [features, other, z_two, below, above]
        far_early = [swap_core(v) for v in near_early]
        across = [move_z(below[:half], 1), move_z(above[half:], -1)]
    with jax.named_scope("aggregate"):
        places = ((0, 4), (4, 4), (8, 6), (14, 4), (18, 4))
        places += tuple((22 + at, n) for at, n in places)
        (early_sum,) = tile_product(
            values, col_src, row_at, forward_plan, 0, near_early + far_early,
            [[(0, at, n)] for at, n in places], ((0, 16),), False, 44,
        )
    with jax.named_scope("gather_features"):
        *across, y_two, early_sum = lax.optimization_barrier((*across, y_two, early_sum))
        near_late = [cat(*across), y_two]
        cotangent_in, _ = lax.optimization_barrier((cotangent, y_two))
        other_cotangent = swap_f(cotangent_in)
        far_late = [swap_core(v) for v in near_late]
    with jax.named_scope("aggregate"):
        places = ((0, 4), (4, 6), (10, 4), (14, 6))
        own, ahead, across, behind = tile_product(
            values, col_src, row_at, forward_plan, 1, near_late + far_late,
            [[(0, at, n)] for at, n in places],
            ((0, 4), (4, 4), (8, 4), (12, 4)), False, 44, early_sum,
        )
    with jax.named_scope("sum_over_col"):
        own, ahead, across, behind = [v.reshape(512, 256) for v in (own, ahead, across, behind)]
        across, ahead, behind, other_cotangent = lax.optimization_barrier(
            (across, ahead, behind, other_cotangent)
        )
        weight_in, own = lax.optimization_barrier((weight, own))
        far_up, far_down = move_x(across[:half], 1), move_x(across[half:], -1)
        other_weight = swap_f(weight_in)
        ahead = move_x(cat(ahead[:half] + far_up, ahead[half:]), 1)
        behind = move_x(cat(behind[:half], behind[half:] + far_down), -1)
        agg = own + ahead + behind
        agg, other_weight = lax.optimization_barrier((agg, other_weight))
    with jax.named_scope("activate"):
        other_agg = swap_f(cat(agg[half:], agg[:half]))
        pre_act = (
            jnp.dot(agg, weight, precision=HIGH)
            + jnp.dot(other_agg, other_weight, precision=HIGH)
            + out_bias
        )
        sigmoid_pre = jax.nn.sigmoid(pre_act)
        activated = (pre_act * sigmoid_pre)[:half]
        both = cat(cotangent, other_cotangent)
        slope = both * (sigmoid_pre * (1.0 + pre_act * (1.0 - sigmoid_pre)))
        back = jnp.einsum("no,fo->nf", slope, weight, precision=HIGH)
    with jax.named_scope("gather_back"):
        ring = [back] + [move_x(back, -d) for d in (1, 2, 3)]
    with jax.named_scope("weight_gradient"):
        slope, agg, back = lax.optimization_barrier((slope, agg, back))
        gw = jnp.einsum("nf,no->fo", agg, slope, precision=HIGH)
        gw = lax.all_to_all(gw, "row", 0, 0, tiled=True)
        gw = jnp.sum(gw.reshape(16, 16, 512), axis=0)
        gw, ring[0] = lax.optimization_barrier((gw, back))
    with jax.named_scope("back_tile"):
        near_two_0, near_two_1, far_two_0, far_two_1, near_one, far_one = tile_product(
            values, row_at, col_dst, backward_plan, 0, ring,
            [[(0, 4 * i, 4)] for i in range(4)],
            ((0, 8), (8, 8), (16, 8), (24, 8), (32, 16), (48, 16)), True, 30,
        )
    with jax.named_scope("sum_over_row"):
        far_one = swap_core(far_one.reshape(4, 512, 256))
        far_two_1, far_two_0, far_one = lax.optimization_barrier((far_two_1, far_two_0, far_one))
        near_one = near_one.reshape(4, 512, 256)
        one = [near_one[d] + far_one[d] for d in range(4)]
        far_two_1 = swap_core(far_two_1.reshape(4, 256, 256))
        far_two_0 = swap_core(far_two_0.reshape(4, 256, 256))
        gw, near_two_1, *one = lax.optimization_barrier((gw, near_two_1, *one))
        two_1 = swap_y(near_two_1.reshape(4, 256, 256) + far_two_1)
        one = [one[0], move_z(one[1], 1), move_z(one[3], -1), move_z(one[2], 2)]
    with jax.named_scope("weight_gradient"):
        gw = jnp.broadcast_to(gw[None], (4, 16, 512)).reshape(64, 512)
        gw = lax.all_to_all(gw, "col", 0, 0, tiled=True)
        gw = jnp.sum(gw.reshape(4, 16, 512), axis=0)
        gw = jnp.broadcast_to(gw[None], (16, 16, 512)).reshape(256, 512)
        grad_weight = lax.all_to_all(gw, "row", 0, 0, tiled=True)
        grad_weight, two_1 = lax.optimization_barrier((grad_weight, two_1))
    with jax.named_scope("sum_over_row"):
        two = two_1 + (near_two_0.reshape(4, 256, 256) + far_two_0)
        one = one[0] + one[1] + one[2] + one[3]
        one, two = lax.optimization_barrier((one, two))
        two = two[0] + move_z(two[1], 1) + move_z(two[3], -1) + move_z(two[2], 2)
        grad_features = cat(one[:half] + swap_y(one[half:]), two)
    return activated, grad_features, grad_weight


def solution(mesh):
    return jax.shard_map(
        on_device,
        mesh=mesh,
        in_specs=(
            P("row", "col", None, None, None),
            P("row", "col", None),
            P("row", "col", None),
            P("row", "col"),
            P(("col", "row"), "feat"),
            P("feat", None),
            P(),
            P(("row", "col", "feat"), None),
        ),
        out_specs=(P(("row", "col", "feat"), None), P(("col", "row"), "feat"), P("feat", None)),
        check_vma=False,
    )
```

```python
import functools

import jax
import jax.numpy as jnp
from jax import lax
from jax.experimental import pallas as pl
from jax.experimental.pallas import tpu as pltpu
from jax.sharding import PartitionSpec as P

BLK = 128
PER_STEP = 48
HIGH = lax.Precision.HIGH

Y, Z, C = 2, 4, 2


def row_perm(dy, dz, dc):
    pairs = []
    for y in range(Y):
        for z in range(Z):
            for c in range(C):
                there = ((y + dy) % Y) * 8 + ((z + dz) % Z) * 2 + (c + dc) % C
                pairs.append((y * 8 + z * 2 + c, there))
    return pairs


def move_z(v, dz):
    return lax.ppermute(v, "row", row_perm(0, dz, 0))


def swap_y(v):
    return lax.ppermute(v, "row", row_perm(1, 0, 0))


def swap_core(v):
    return lax.ppermute(v, "row", row_perm(0, 0, 1))


def move_x(v, dx):
    return lax.ppermute(v, "col", [(x, (x + dx) % 4) for x in range(4)])


def swap_f(v):
    return lax.ppermute(v, "feat", [(0, 1), (1, 0)])


def cat(*parts):
    return jnp.concatenate(parts, axis=0)


def split(v):
    hi = v.astype(jnp.bfloat16)
    lo = (v - hi.astype(jnp.float32)).astype(jnp.bfloat16)
    return hi, lo


def order_slots(group, live):
    key = jnp.where(live, group, 2).reshape(-1, PER_STEP).astype(jnp.int32)
    place = jnp.arange(PER_STEP, dtype=jnp.int32)
    before = (key[:, None, :] < key[:, :, None]) | (
        (key[:, None, :] == key[:, :, None]) & (place[None, None, :] < place[None, :, None])
    )
    rank = jnp.sum(before, axis=2, dtype=jnp.int32)
    order = jnp.sum(
        jnp.where(rank[:, None, :] == place[None, :, None], place[None, None, :], 0),
        axis=2,
        dtype=jnp.int32,
    )
    zero = jnp.zeros(key.shape[0], jnp.int32)
    first = jnp.sum(key == 0, axis=1, dtype=jnp.int32)
    both = jnp.sum(key <= 1, axis=1, dtype=jnp.int32)
    return order.reshape(-1), jnp.concatenate([zero, first, both])


def tile_kernel(steps, transpose, places, targets, bounds_at, carried, *refs):
    src, dst, order, bounds, a_ref = refs[:5]
    x_refs = refs[5 : 5 + len(places)]
    init = refs[5 + len(places)] if carried else None
    at = 5 + len(places) + int(carried)
    o_refs = refs[at : at + len(targets)]
    xcat, acc, sems = refs[at + len(targets) :]
    step = pl.program_id(0)

    @pl.when(step == 0)
    def _():
        if carried:
            acc[...] = init[...]
        else:
            acc[...] = jnp.zeros_like(acc)
        for x_ref, spans in zip(x_refs, places):
            for first, to, n in spans:

                def convert(i, carry, x_ref=x_ref, first=first, to=to):
                    hi, lo = split(x_ref[first + i])
                    xcat[to + i, 0:128, :] = hi
                    xcat[to + i, 128:256, :] = hi
                    xcat[to + i, 256:384, :] = lo
                    return carry

                lax.fori_loop(0, n, convert, 0, unroll=min(n, 4))

    begin = bounds[bounds_at * steps + step]
    end = bounds[(bounds_at + 1) * steps + step]
    base = step * PER_STEP

    def group(first, size):
        for u in range(size):
            p = first + u
            live = p < end
            slot = order[base + jnp.minimum(p, PER_STEP - 1)]
            r = jnp.where(live, dst[base + slot], 0)
            c = jnp.where(live, src[base + slot], 0)
            a = jnp.where(live, a_ref[slot], 0.0)
            if transpose:
                a = a.T
            hi, lo = split(a)
            lhs = jnp.concatenate([hi, lo, hi], axis=1)
            acc[r] = acc[r] + jnp.dot(lhs, xcat[c], preferred_element_type=jnp.float32)

    full = lax.div(end - begin + 9, 16)
    rest = begin + full * 16

    def large(g, carry):
        group(begin + g * 16, 16)
        return carry

    def small(g, carry):
        group(rest + g * 4, 4)
        return carry

    lax.fori_loop(0, full, large, 0)
    lax.fori_loop(0, lax.div(jnp.maximum(end - rest, 0) + 3, 4), small, 0)

    @pl.when(step == steps - 1)
    def _():
        copies = [
            pltpu.make_async_copy(acc.at[pl.ds(first, n)], o_ref, sems.at[i])
            for i, (o_ref, (first, n)) in enumerate(zip(o_refs, targets))
        ]
        for copy in copies:
            copy.start()
        for copy in copies:
            copy.wait()


def tile_product(values, src, dst, plan, part, pieces, places, targets, transpose, limit, init=None):
    order, bounds = plan
    slots = values.shape[0]
    steps = slots // PER_STEP
    width = pieces[0].shape[-1]
    pieces = [p.reshape(-1, BLK, width) for p in pieces]
    n_src = max(to + n for spans in places for _, to, n in spans)
    n_dst = max(first + n for first, n in targets)
    inits = [] if init is None else [init]

    def whole(shape):
        return pl.BlockSpec(shape, lambda i, *_: (0, 0, 0), pipeline_mode=pl.Buffered(1))

    return pl.pallas_call(
        functools.partial(
            tile_kernel, steps, transpose, places, targets, part, init is not None
        ),
        grid_spec=pltpu.PrefetchScalarGridSpec(
            num_scalar_prefetch=4,
            grid=(steps,),
            in_specs=[pl.BlockSpec((PER_STEP, BLK, BLK), lambda i, *_: (i, 0, 0))]
            + [whole(p.shape) for p in pieces + inits],
            out_specs=[pl.BlockSpec(memory_space=pl.ANY) for _ in targets],
            scratch_shapes=[
                pltpu.VMEM((n_src, 3 * BLK, width), jnp.bfloat16),
                pltpu.VMEM((n_dst, BLK, width), jnp.float32),
                pltpu.SemaphoreType.DMA((len(targets),)),
            ],
        ),
        out_shape=[jax.ShapeDtypeStruct((n, BLK, width), jnp.float32) for _, n in targets],
        compiler_params=pltpu.CompilerParams(vmem_limit_bytes=limit << 20),
        cost_estimate=pl.CostEstimate(
            flops=slots * BLK * 3 * BLK * width,
            bytes_accessed=slots * BLK * BLK * 4 + (n_src + n_dst) * BLK * width * 4,
            transcendentals=0,
        ),
    )(src, dst, order, bounds, values, *pieces, *inits)


def on_device(
    block_values, block_rows, block_cols, block_count, features, weight, out_bias, cotangent
):
    values = block_values[0, 0]
    live = jnp.arange(values.shape[0], dtype=jnp.int32) < block_count[0, 0]
    row, x, f = lax.axis_index("row"), lax.axis_index("col"), lax.axis_index("feat")
    y, z, core = row // 8, (row // 2) % 4, row % 2

    cols = jnp.clip(block_cols[0, 0], 0, 63)
    rows = jnp.clip(block_rows[0, 0], 0, 15)
    owner = cols // 4
    dc, dy, dz, blk = (owner % 2) ^ core, (owner // 8) ^ y, ((owner // 2) - z) & 3, cols % 4
    dx, df = ((rows // 4) - x) & 3, ((rows // 2) % 2) ^ f
    row_at = dx * 4 + df * 2 + rows % 2

    early = (dz == 0) | ((dy == 0) & (blk >= 2)) | ((dz != 2) & (blk < 2))
    seq = jnp.where(dz == 3, 0, dz)
    col_early = dc * 22 + jnp.where(
        dz == 0, dy * 4 + blk, jnp.where(blk >= 2, 8 + seq * 2 + blk - 2, 14 + seq * 4 + dy * 2 + blk)
    )
    col_late = dc * 10 + jnp.where(blk >= 2, 4 + seq * 2 + blk - 2, dy * 2 + blk)
    col_src = jnp.where(early, col_early, col_late)
    forward_plan = order_slots(jnp.where(early, 0, 1), live)

    col_dst = dc * 16 + jnp.where(blk >= 2, dy * 8 + dz * 2 + blk - 2, 32 + dz * 4 + dy * 2 + blk)
    backward_plan = order_slots(jnp.zeros_like(rows), live)

    half = 256
    with jax.named_scope("gather_features"):
        other = swap_y(features)
        second, forward_order = lax.optimization_barrier((features[half:], forward_plan[0]))
        forward_plan = (forward_order, forward_plan[1])
        z_two = cat(*[move_z(second, d) for d in (1, -1, 2)])
        y_two = swap_y(z_two)
        pair = cat(features[:half], other[:half])
        below, above = move_z(pair, 1), move_z(pair, -1)
        near_early = [features, other, z_two, below, above]
        far_early = [swap_core(v) for v in near_early]
        across = [move_z(below[:half], 1), move_z(above[half:], -1)]
    with jax.named_scope("aggregate"):
        places = ((0, 4), (4, 4), (8, 6), (14, 4), (18, 4))
        places += tuple((22 + at, n) for at, n in places)
        (early_sum,) = tile_product(
            values, col_src, row_at, forward_plan, 0, near_early + far_early,
            [[(0, at, n)] for at, n in places], ((0, 16),), False, 44,
        )
    with jax.named_scope("gather_features"):
        *across, y_two, early_sum = lax.optimization_barrier((*across, y_two, early_sum))
        near_late = [cat(*across), y_two]
        cotangent_in, _ = lax.optimization_barrier((cotangent, y_two))
        other_cotangent = swap_f(cotangent_in)
        far_late = [swap_core(v) for v in near_late]
    with jax.named_scope("aggregate"):
        places = ((0, 4), (4, 6), (10, 4), (14, 6))
        own, ahead, across, behind = tile_product(
            values, col_src, row_at, forward_plan, 1, near_late + far_late,
            [[(0, at, n)] for at, n in places],
            ((0, 4), (4, 4), (8, 4), (12, 4)), False, 44, early_sum,
        )
    with jax.named_scope("sum_over_col"):
        own, ahead, across, behind = [v.reshape(512, 256) for v in (own, ahead, across, behind)]
        weight_in, own = lax.optimization_barrier((weight, own))
        far_up, far_down = move_x(across[:half], 1), move_x(across[half:], -1)
        other_weight = swap_f(weight_in)
        far_up, far_down, other_cotangent = lax.optimization_barrier(
            (far_up, far_down, other_cotangent)
        )
        ahead = move_x(cat(ahead[:half] + far_up, ahead[half:]), 1)
        behind = move_x(cat(behind[:half], behind[half:] + far_down), -1)
        agg = own + ahead + behind
        agg, other_weight = lax.optimization_barrier((agg, other_weight))
    with jax.named_scope("activate"):
        other_agg = swap_f(cat(agg[half:], agg[:half]))
        pre_act = (
            jnp.dot(agg, weight, precision=HIGH)
            + jnp.dot(other_agg, other_weight, precision=HIGH)
            + out_bias
        )
        sigmoid_pre = jax.nn.sigmoid(pre_act)
        activated = (pre_act * sigmoid_pre)[:half]
        both = cat(cotangent, other_cotangent)
        slope = both * (sigmoid_pre * (1.0 + pre_act * (1.0 - sigmoid_pre)))
        back = jnp.einsum("no,fo->nf", slope, weight, precision=HIGH)
    with jax.named_scope("gather_back"):
        ring = [back] + [move_x(back, -d) for d in (1, 2, 3)]
    with jax.named_scope("weight_gradient"):
        slope, agg, back = lax.optimization_barrier((slope, agg, back))
        gw = jnp.einsum("nf,no->fo", agg, slope, precision=HIGH)
        gw = lax.all_to_all(gw, "row", 0, 0, tiled=True)
        gw = jnp.sum(gw.reshape(16, 16, 512), axis=0)
        gw, ring[0] = lax.optimization_barrier((gw, back))
    with jax.named_scope("back_tile"):
        near_two_0, near_two_1, far_two_0, far_two_1, near_one, far_one = tile_product(
            values, row_at, col_dst, backward_plan, 0, ring,
            [[(0, 4 * i, 4)] for i in range(4)],
            ((0, 8), (8, 8), (16, 8), (24, 8), (32, 16), (48, 16)), True, 30,
        )
    with jax.named_scope("sum_over_row"):
        far_one = swap_core(far_one.reshape(4, 512, 256))
        far_two_1, far_two_0, far_one = lax.optimization_barrier((far_two_1, far_two_0, far_one))
        near_one = near_one.reshape(4, 512, 256)
        one = [near_one[d] + far_one[d] for d in range(4)]
        far_two_1 = swap_core(far_two_1.reshape(4, 256, 256))
        far_two_0 = swap_core(far_two_0.reshape(4, 256, 256))
        gw, near_two_1, *one = lax.optimization_barrier((gw, near_two_1, *one))
        near_two_1, far_two_0 = lax.optimization_barrier((near_two_1, far_two_0))
        two_1 = swap_y(near_two_1.reshape(4, 256, 256) + far_two_1)
        one = [one[0], move_z(one[1], 1), move_z(one[3], -1), move_z(one[2], 2)]
    with jax.named_scope("weight_gradient"):
        gw = jnp.broadcast_to(gw[None], (4, 16, 512)).reshape(64, 512)
        gw = lax.all_to_all(gw, "col", 0, 0, tiled=True)
        gw = jnp.sum(gw.reshape(4, 16, 512), axis=0)
        gw = jnp.broadcast_to(gw[None], (16, 16, 512)).reshape(256, 512)
        grad_weight = lax.all_to_all(gw, "row", 0, 0, tiled=True)
        grad_weight, two_1 = lax.optimization_barrier((grad_weight, two_1))
    with jax.named_scope("sum_over_row"):
        two = two_1 + (near_two_0.reshape(4, 256, 256) + far_two_0)
        one = one[0] + one[1] + one[2] + one[3]
        one, two = lax.optimization_barrier((one, two))
        two = two[0] + move_z(two[1], 1) + move_z(two[3], -1) + move_z(two[2], 2)
        grad_features = cat(one[:half] + swap_y(one[half:]), two)
    return activated, grad_features, grad_weight


def solution(mesh):
    return jax.shard_map(
        on_device,
        mesh=mesh,
        in_specs=(
            P("row", "col", None, None, None),
            P("row", "col", None),
            P("row", "col", None),
            P("row", "col"),
            P(("col", "row"), "feat"),
            P("feat", None),
            P(),
            P(("row", "col", "feat"), None),
        ),
        out_specs=(P(("row", "col", "feat"), None), P(("col", "row"), "feat"), P("feat", None)),
        check_vma=False,
    )
```
